256 devices in a mesh: section: 64 (over x, y_hi, z), tensor: 4 (over y_lo, core).
Axes of the slice: x: 4, y: 4 (y_hi: 2, y_lo: 2; y = y_hi * 2 + y_lo), z: 8, core: 2. Of those that a mesh axis runs over, the one named last changes fastest.
Arguments:
- state: bfloat16 [64, 16, 2560], P('section'), may hold values from -6 to 6
- gain_in: bfloat16 [64, 2560], P('section'), may hold values from 0.25 to 1.75
- w_query: bfloat16 [64, 2560, 4096], P('section', None, 'tensor'), may hold values from -0.125 to 0.125
- w_key: bfloat16 [64, 2560, 512], P('section', None, 'tensor'), may hold values from -0.125 to 0.125
- w_value: bfloat16 [64, 2560, 512], P('section', None, 'tensor'), may hold values from -0.125 to 0.125
- w_output: bfloat16 [64, 4096, 2560], P('section', 'tensor'), may hold values from -0.375 to 0.375
- query_gain: bfloat16 [64, 128], P('section'), may hold values from 0.099609375 to 1.8984375
- key_gain: bfloat16 [64, 128], P('section'), may hold values from 0.099609375 to 1.8984375
- cache_keys: bfloat16 [64, 16, 4, 32, 128], P('section', None, 'tensor'), may hold values from -600 to 600
- cache_values: bfloat16 [64, 16, 4, 32, 128], P('section', None, 'tensor'), may hold values from -6 to 6
- lengths: int32 [64, 16], P('section'), may hold values from 4 to 32, as said below
Outputs:
- handed: bfloat16 [64, 16, 2560], P('section')
- new_keys: bfloat16 [64, 16, 4, 128], P('section', None, 'tensor')
- new_values: bfloat16 [64, 16, 4, 128], P('section', None, 'tensor')
The draws below stay inside these ranges and needn't reach their ends.
Inputs may be any that keep to these rules, and one draw needn't show every extreme that they name: `lengths`: in every section at least one row holds 32 tokens.
All inputs are finite; a program needn't handle non-finite values.
Results may differ from the reference program's by a relative error of at most 0.012.
The reference program's roundings to bfloat16 on the way count: a program that leaves them out, or rounds other values in their place, can miss the bound.
Values may be sent and summed in bfloat16 or wider, within the bound.
No kernel may reach another device: no remote copies, remote signals or barrier semaphores. Data moves between devices by JAX's collectives and lax.ppermute only.
A program may use at most 64 MiB of HBM per device.

```python
import math
import jax
import jax.numpy as jnp
from jax import lax

D = 2560
HEADS = 32
KVH = 4
HD = 128
R = 16
CACHE = 32
SECTIONS = 64


def draw_state(key, part):
    key = jax.random.fold_in(key, 11)
    key_noise, key_rows, key_cols = jax.random.split(key, 3)
    row_scale = jnp.exp(jax.random.uniform(key_rows, (SECTIONS, R, 1), minval=math.log(0.02), maxval=math.log(0.2)))
    col_scale = jnp.exp(jax.random.uniform(key_cols, (SECTIONS, 1, D), minval=math.log(0.3), maxval=math.log(3.0)))
    noise = jax.random.normal(key_noise, (SECTIONS, R, D), dtype=jnp.float32)
    return jnp.clip(noise * row_scale * col_scale, -6.0, 6.0).astype(jnp.bfloat16)


def draw_cache_keys(key, part):
    key = jax.random.fold_in(key, 12)
    key_base = jax.random.fold_in(key, 0)
    base = jax.random.normal(key_base, (SECTIONS, R, KVH, CACHE, HD), dtype=jnp.float32)
    return jnp.clip(base, -600.0, 600.0).astype(jnp.bfloat16)


def draw_lengths(key, part):
    key = jax.random.fold_in(key, 13)
    key_base, key_pick = jax.random.split(key, 2)
    filled = jax.random.randint(key_base, (SECTIONS, R), max(1, CACHE // 8), CACHE + 1)
    chosen = jax.random.randint(key_pick, (SECTIONS, 1), 0, R)
    longest = jnp.arange(R)[None, :] == chosen
    return jnp.where(longest, CACHE, filled).astype(jnp.int32)


def level_of(own_key, shape, shards, low, largest):
    loudness, own = 1.0, jax.random.fold_in(own_key, 6)
    for axis_at, parts in shards:
        heights = jnp.exp(jax.random.uniform(jax.random.fold_in(own, axis_at), (parts,), jnp.float32, low / len(shards), largest / len(shards)))
        loudness = loudness * jnp.repeat(heights, shape[axis_at] // parts).reshape([-1 if axis == axis_at else 1 for axis in range(len(shape))])
    return loudness


def normal_values(rng, extent, width, most, cuts=(), kind=jnp.bfloat16):
    entries = jax.random.normal(rng, extent, jnp.float32) * width
    if len(cuts) > 0:
        entries = level_of(rng, extent, cuts, -0.22, 0.18) * entries
    return jnp.clip(entries, min=-most, max=most).astype(kind)


def setup_inputs(seed: int = 0) -> dict:
    seeds = jax.random.split(jax.random.key(seed), 12)
    state = draw_state(jax.random.fold_in(seeds[11], 71), 0)
    gain_in = jnp.clip(1.0 + 0.15 * jax.random.normal(seeds[1], (SECTIONS, D), jnp.float32), 0.25, 1.75).astype(jnp.bfloat16)
    w_query = normal_values(seeds[2], (SECTIONS, D, HEADS * HD), D ** -0.5, 0.125, ((0, 64), (2, 4)))
    w_key = normal_values(seeds[3], (SECTIONS, D, KVH * HD), D ** -0.5, 0.125, ((0, 64), (2, 4)))
    w_value = normal_values(seeds[4], (SECTIONS, D, KVH * HD), D ** -0.5, 0.125, ((0, 64), (2, 4)))
    w_output = normal_values(seeds[5], (SECTIONS, HEADS * HD, D), (HEADS * HD // 16) ** -0.5, 0.375, ((0, 64), (1, 4)))
    query_gain = jnp.clip(1.0 + 0.18 * jax.random.normal(seeds[6], (SECTIONS, HD), jnp.float32), 0.099609375, 1.8984375).astype(jnp.bfloat16)
    key_gain = jnp.clip(1.0 + 0.18 * jax.random.normal(seeds[7], (SECTIONS, HD), jnp.float32), 0.099609375, 1.8984375).astype(jnp.bfloat16)
    cache_keys = draw_cache_keys(jax.random.fold_in(seeds[11], 71), 0)
    cache_values = normal_values(seeds[9], (SECTIONS, R, KVH, CACHE, HD), 1.0, 6.0, ((0, 64), (2, 4)))
    lengths = draw_lengths(jax.random.fold_in(seeds[11], 71), 0)
    return dict(state=state, gain_in=gain_in, w_query=w_query, w_key=w_key, w_value=w_value, w_output=w_output, query_gain=query_gain, key_gain=key_gain, cache_keys=cache_keys, cache_values=cache_values, lengths=lengths)


epsilon = 1e-06
rope_base = 1000000.0

def rms_norm(values, gain_vec):
    return values * lax.rsqrt(lax.optimization_barrier(jnp.mean(values * values, axis=-1, keepdims=True)) + epsilon) * gain_vec.astype(jnp.float32)

def rotate(values, position):
    half_dim = values.shape[-1] // 2
    frequency = rope_base ** (-(jnp.arange(half_dim, dtype=jnp.float32) * 2.0 / values.shape[-1]))
    angles = position.astype(jnp.float32)[:, None] * frequency[None, :]
    target_shape = (angles.shape[0],) + (1,) * (values.ndim - 2) + (half_dim,)
    cosine = jnp.cos(angles).reshape(target_shape)
    sine = jnp.sin(angles).reshape(target_shape)
    lower_half = values[..., :half_dim]
    upper_half = values[..., half_dim:]
    return jnp.concatenate([lower_half * cosine - upper_half * sine, upper_half * cosine + lower_half * sine], axis=-1)

def section_tick(hidden_in, gain_in, w_query, w_key, w_value, w_output, query_gain, key_gain, cache_key, cache_val, lengths):
    row_count = hidden_in.shape[0]
    kv_heads = w_key.shape[1] // HD
    head_group = w_query.shape[1] // w_key.shape[1]
    normed = rms_norm(hidden_in.astype(jnp.float32), gain_in).astype(jnp.bfloat16)
    query = jnp.dot(normed, w_query, preferred_element_type=jnp.float32).reshape(row_count, kv_heads, head_group, HD)
    key_raw = jnp.dot(normed, w_key, preferred_element_type=jnp.float32).reshape(row_count, kv_heads, HD)
    new_value = jnp.dot(normed, w_value, preferred_element_type=jnp.float32).astype(jnp.bfloat16).reshape(row_count, kv_heads, HD)
    query_rot = rotate(rms_norm(query, query_gain), lengths).astype(jnp.bfloat16)
    new_key = rotate(rms_norm(key_raw, key_gain), lengths).astype(jnp.bfloat16)
    score_scale = HD ** (-0.5)
    cache_score = jnp.einsum('rkgd,rkjd->rkgj', query_rot.astype(jnp.float32), cache_key.astype(jnp.float32)) * score_scale
    own_score = jnp.einsum('rkgd,rkd->rkg', query_rot.astype(jnp.float32), new_key.astype(jnp.float32)) * score_scale
    in_cache = jnp.arange(cache_key.shape[2])[None, None, None, :] < lengths[:, None, None, None]
    masked = jnp.where(in_cache, cache_score, -1e+30)
    row_max = jnp.maximum(lax.optimization_barrier(jnp.max(masked, axis=-1)), own_score)
    cache_exp = jnp.where(in_cache, jnp.exp(masked - row_max[..., None]), 0.0)
    own_exp = jnp.exp(own_score - row_max)
    denom_sum = lax.optimization_barrier(jnp.sum(cache_exp, axis=-1)) + own_exp
    cache_prob = (cache_exp / denom_sum[..., None]).astype(jnp.bfloat16)
    own_prob = (own_exp / denom_sum).astype(jnp.bfloat16)
    attended = jnp.einsum('rkgj,rkjd->rkgd', cache_prob.astype(jnp.float32), cache_val.astype(jnp.float32))
    attended = attended + own_prob.astype(jnp.float32)[..., None] * new_value.astype(jnp.float32)[:, :, None, :]
    attended = attended.astype(jnp.bfloat16).reshape(row_count, kv_heads * head_group * HD)
    result = (hidden_in.astype(jnp.float32) + jnp.dot(attended, w_output, preferred_element_type=jnp.float32)).astype(jnp.bfloat16)
    return (result, new_key, new_value)

def reference(state, gain_in, w_query, w_key, w_value, w_output, query_gain, key_gain, cache_keys, cache_values, lengths):

    def per_section(section_items):
        return section_tick(*section_items)
    result, new_keys, new_values = lax.map(per_section, (state, gain_in, w_query, w_key, w_value, w_output, query_gain, key_gain, cache_keys, cache_values, lengths))
    handed = jnp.roll(result, 1, axis=0)
    return (handed, new_keys, new_values)
```

```python
import functools

import jax
import jax.numpy as jnp
from jax import lax
from jax.experimental import pallas as pl
from jax.experimental.pallas import tpu as pltpu
from jax.sharding import PartitionSpec as P

HD = 128
EPSILON = 1e-06
LOG_BASE = 13.815510557964274
NEG = -1e30
F32 = jnp.float32
BF16 = jnp.bfloat16


def dot(a, b):
    return jnp.dot(a, b, preferred_element_type=F32)


def kernel(
    state, gain, wq, wk, wv, wo, qgain, kgain, ckey, cval, lens,
    part, newk, newv,
    state_v, gain_v, wq_v, wkv_v, wo_v, qgain_v, kgain_v, key_v, val_v, lens_v,
    sem, wq_sem, wo_sem,
):
    rows, width = state_v.shape[1:]
    slots = ckey.shape[1]
    cached = rows * slots
    group = wq.shape[2] // HD
    wq_parts, wo_parts = wq_sem.shape[0], wo_sem.shape[0]
    wq_rows, wo_rows = wq.shape[1] // wq_parts, wo.shape[1] // wo_parts

    def copy(src, dst, s):
        c = pltpu.make_async_copy(src, dst, s)
        c.start()
        return c

    c_state = copy(state, state_v, sem.at[0])
    c_gain = copy(gain, gain_v, sem.at[1])
    c_lens = copy(lens, lens_v, sem.at[2])
    c_qgain = copy(qgain, qgain_v, sem.at[3])
    c_kgain = copy(kgain, kgain_v, sem.at[4])
    c_wk = copy(wk.at[0], wkv_v.at[:, pl.ds(0, HD)], sem.at[5])
    c_wv = copy(wv.at[0], wkv_v.at[:, pl.ds(HD, HD)], sem.at[6])
    c_wq = [
        copy(wq.at[0, pl.ds(i * wq_rows, wq_rows)], wq_v.at[pl.ds(i * wq_rows, wq_rows)], wq_sem.at[i])
        for i in range(wq_parts)
    ]
    c_key = copy(ckey, key_v, sem.at[7])
    c_val = copy(cval, val_v, sem.at[8])
    c_wo = [
        copy(wo.at[0, pl.ds(i * wo_rows, wo_rows)], wo_v.at[pl.ds(i * wo_rows, wo_rows)], wo_sem.at[i])
        for i in range(wo_parts)
    ]

    c_lens.wait()
    row_i = lax.broadcasted_iota(jnp.int32, (rows, rows), 0)
    row_j = lax.broadcasted_iota(jnp.int32, (rows, rows), 1)
    length = jnp.sum(
        jnp.where(row_i == row_j, lens_v[...].astype(F32), 0.0), axis=1, keepdims=True
    )
    lane = lax.broadcasted_iota(jnp.int32, (rows, HD), 1)
    half = lax.rem(lane, HD // 2).astype(F32)
    angle = length * jnp.exp(half * (-2.0 * LOG_BASE / HD))
    cosine = jnp.cos(angle)
    sine = jnp.sin(angle)
    sine = jnp.where(lane < HD // 2, -sine, sine)

    c_state.wait()
    c_gain.wait()
    hidden = state_v[0].astype(F32)
    mean = jnp.mean(hidden * hidden, axis=-1, keepdims=True)
    normed = (hidden * lax.rsqrt(mean + EPSILON) * gain_v[...].astype(F32)).astype(BF16)

    def head_norm(x, gain_row):
        mean = jnp.mean(x * x, axis=-1, keepdims=True)
        x = x * lax.rsqrt(mean + EPSILON) * gain_row
        return (x * cosine + pltpu.roll(x, HD // 2, 1) * sine).astype(BF16)

    c_wk.wait()
    c_wv.wait()
    c_kgain.wait()
    key_value = dot(normed, wkv_v[...])
    new_key = head_norm(key_value[:, :HD], kgain_v[...].astype(F32))
    new_value = key_value[:, HD:].astype(BF16)
    newk[...] = new_key
    newv[...] = new_value

    query = jnp.zeros((rows, group * HD), F32)
    for i in range(wq_parts):
        c_wq[i].wait()
        at = i * wq_rows
        query = query + dot(normed[:, at : at + wq_rows], wq_v[at : at + wq_rows])
    c_qgain.wait()
    qgain_row = qgain_v[...].astype(F32)
    query_rot = jnp.concatenate(
        [head_norm(query[:, g * HD : (g + 1) * HD], qgain_row) for g in range(group)], axis=0
    )

    count = group * rows
    c_key.wait()
    last = (((1,), (1,)), ((), ()))
    pad = jnp.zeros((HD - rows, HD), BF16)
    keys = jnp.concatenate([key_v[...].reshape(cached, HD), new_key, pad], axis=0)
    scores = lax.dot_general(query_rot, keys, last, preferred_element_type=F32) * HD**-0.5
    spread = cached + HD
    at_row = lax.broadcasted_iota(jnp.int32, (rows, spread), 0)
    at_col = lax.broadcasted_iota(jnp.int32, (rows, spread), 1)
    slot = at_col - at_row * slots
    length_i = length.astype(jnp.int32)
    valid = ((slot >= 0) & (slot < length_i) & (at_col < cached)) | (at_col == cached + at_row)
    valid = jnp.where(valid, 1.0, 0.0)
    valid = jnp.concatenate([valid] * group, axis=0) > 0.5
    masked = jnp.where(valid, scores, NEG)
    top = jnp.max(masked, axis=-1, keepdims=True)
    weight = jnp.exp(masked - top)
    total = jnp.sum(weight, axis=-1, keepdims=True)
    probs = (weight * (1.0 / total)).astype(BF16)
    c_val.wait()
    values = jnp.concatenate([val_v[...].reshape(cached, HD), new_value, pad], axis=0)
    attended = dot(probs, values).astype(BF16)
    attended = jnp.concatenate([attended[g * rows : (g + 1) * rows] for g in range(group)], axis=1)

    first = lax.axis_index("tensor") == 0
    out = jnp.where(first, hidden, 0.0)
    for i in range(wo_parts):
        c_wo[i].wait()
        at = i * wo_rows
        out = out + dot(attended[:, at : at + wo_rows], wo_v[at : at + wo_rows])
    part[...] = out.astype(BF16)


def section_partial(args):
    state, gain, wq, wk, wv, wo, qgain, kgain, ckey, cval, lens = args
    rows, width = state.shape[1:]
    wq_parts, wo_parts = 10, 4
    any_space = pl.BlockSpec(memory_space=pltpu.HBM)
    vmem = pl.BlockSpec(memory_space=pltpu.VMEM)
    slots = ckey.shape[3]
    ckey = ckey.reshape(rows, slots, HD)
    cval = cval.reshape(rows, slots, HD)
    args = (state, gain, wq, wk, wv, wo, qgain, kgain, ckey, cval, lens)
    return pl.pallas_call(
        kernel,
        out_shape=(
            jax.ShapeDtypeStruct((rows, width), BF16),
            jax.ShapeDtypeStruct((rows, HD), BF16),
            jax.ShapeDtypeStruct((rows, HD), BF16),
        ),
        in_specs=[any_space] * len(args),
        out_specs=(vmem, vmem, vmem),
        scratch_shapes=[
            pltpu.VMEM(state.shape, BF16),
            pltpu.VMEM(gain.shape, BF16),
            pltpu.VMEM(wq.shape[1:], BF16),
            pltpu.VMEM((width, 2 * HD), BF16),
            pltpu.VMEM(wo.shape[1:], BF16),
            pltpu.VMEM(qgain.shape, BF16),
            pltpu.VMEM(kgain.shape, BF16),
            pltpu.VMEM(ckey.shape, BF16),
            pltpu.VMEM(cval.shape, BF16),
            pltpu.VMEM(lens.shape, jnp.int32),
            pltpu.SemaphoreType.DMA((9,)),
            pltpu.SemaphoreType.DMA((wq_parts,)),
            pltpu.SemaphoreType.DMA((wo_parts,)),
        ],
        compiler_params=pltpu.CompilerParams(vmem_limit_bytes=60 * 2**20),
        cost_estimate=pl.CostEstimate(
            flops=2 * rows * (wq.size + wk.size + wv.size + wo.size),
            bytes_accessed=2 * (wq.size + wk.size + wv.size + wo.size + ckey.size + cval.size),
            transcendentals=0,
        ),
    )(*args)


def body(sections, tensors, *args):
    def moved(x, step, flip):
        pairs = [
            (s * tensors + t, (s + step) % sections * tensors + (t ^ flip))
            for s in range(sections)
            for t in range(tensors)
        ]
        return lax.ppermute(x, ("section", "tensor"), pairs)

    part, new_key, new_value = section_partial(args)
    pair = (part.astype(F32) + moved(part, 0, 1).astype(F32)).astype(BF16)
    near, far = moved(pair, 1, 0), moved(pair, 1, 2)
    handed = (near.astype(F32) + far.astype(F32)).astype(BF16)
    rows = part.shape[0]
    return handed[None], new_key.reshape(1, rows, 1, HD), new_value.reshape(1, rows, 1, HD)


def solution(mesh):
    placed = (
        P("section", None, None),
        P("section", None),
        P("section", None, "tensor"),
        P("section", None, "tensor"),
        P("section", None, "tensor"),
        P("section", "tensor", None),
        P("section", None),
        P("section", None),
        P("section", None, "tensor", None, None),
        P("section", None, "tensor", None, None),
        P("section", None),
    )
    return jax.shard_map(
        functools.partial(body, mesh.shape["section"], mesh.shape["tensor"]),
        mesh=mesh,
        in_specs=placed,
        out_specs=(
            P("section", None, None),
            P("section", None, "tensor", None),
            P("section", None, "tensor", None),
        ),
        check_vma=False,
    )
```

```python
import functools

import jax
import jax.numpy as jnp
from jax import lax
from jax.experimental import pallas as pl
from jax.experimental.pallas import tpu as pltpu
from jax.sharding import PartitionSpec as P

HD = 128
EPSILON = 1e-06
BLOCKS = 2
LOG_BASE = 13.815510557964274
NEG = -1e30
F32 = jnp.float32
BF16 = jnp.bfloat16


def dot(a, b):
    return jnp.dot(a, b, preferred_element_type=F32)


def kernel(
    state, gain, wq, wk, wv, wo, qgain, kgain, ckey, cval, lens,
    part, newk, newv,
    state_v, gain_v, wq_v, wkv_v, wo_v, qgain_v, kgain_v, key_v, val_v, lens_v, newk_v, newv_v,
    sem, wq_sem, wo_sem,
):
    rows, width = state_v.shape[1:]
    slots = ckey.shape[1]
    cached = rows * slots
    heads = wq.shape[2] // HD
    blocks = wq_sem.shape[0]
    group = heads // blocks
    span = group * HD
    last = (((1,), (1,)), ((), ()))

    def copy(src, dst, s):
        c = pltpu.make_async_copy(src, dst, s)
        c.start()
        return c

    c_state = copy(state, state_v, sem.at[0])
    c_gain = copy(gain, gain_v, sem.at[1])
    c_lens = copy(lens, lens_v, sem.at[2])
    c_qgain = copy(qgain, qgain_v, sem.at[3])
    c_kgain = copy(kgain, kgain_v, sem.at[4])
    c_wk = copy(wk.at[0], wkv_v.at[:, pl.ds(0, HD)], sem.at[5])
    c_wv = copy(wv.at[0], wkv_v.at[:, pl.ds(HD, HD)], sem.at[6])
    c_key = copy(ckey, key_v, sem.at[7])
    c_val = copy(cval, val_v, sem.at[8])
    c_wq = [copy(wq.at[0, :, pl.ds(i * span, span)], wq_v.at[i], wq_sem.at[i]) for i in range(blocks)]
    c_wo = []

    def start_wo():
        i = len(c_wo)
        at = pl.ds(i * span, span)
        c_wo.append(copy(wo.at[0, at], wo_v.at[at], wo_sem.at[i]))

    c_lens.wait()
    c_state.wait()
    c_gain.wait()
    c_qgain.wait()
    c_kgain.wait()
    row_i = lax.broadcasted_iota(jnp.int32, (rows, rows), 0)
    row_j = lax.broadcasted_iota(jnp.int32, (rows, rows), 1)
    length = jnp.sum(
        jnp.where(row_i == row_j, lens_v[...].astype(F32), 0.0), axis=1, keepdims=True
    )
    lane = lax.broadcasted_iota(jnp.int32, (rows, HD), 1)
    half = lax.rem(lane, HD // 2).astype(F32)
    angle = length * jnp.exp(half * (-2.0 * LOG_BASE / HD))
    cosine = jnp.cos(angle)
    sine = jnp.sin(angle)
    sine = jnp.where(lane < HD // 2, -sine, sine)
    spread = cached + HD
    at_row = lax.broadcasted_iota(jnp.int32, (rows, spread), 0)
    at_col = lax.broadcasted_iota(jnp.int32, (rows, spread), 1)
    slot = at_col - at_row * slots
    valid = (slot >= 0) & (slot < length.astype(jnp.int32)) & (at_col < cached)
    valid = valid | (at_col == cached + at_row)
    bias = jnp.where(valid, 0.0, NEG)

    hidden = state_v[0].astype(F32)
    mean = jnp.mean(hidden * hidden, axis=-1, keepdims=True)
    normed = (hidden * lax.rsqrt(mean + EPSILON) * gain_v[...].astype(F32)).astype(BF16)
    qgain_row = qgain_v[...].astype(F32)

    def head_norm(x, gain_row):
        mean = jnp.mean(x * x, axis=-1, keepdims=True)
        x = x * lax.rsqrt(mean + EPSILON) * gain_row
        return (x * cosine + pltpu.roll(x, HD // 2, 1) * sine).astype(BF16)

    c_wk.wait()
    c_wv.wait()
    key_value = dot(normed, wkv_v[...])
    new_key = head_norm(key_value[:, :HD], kgain_v[...].astype(F32))
    new_value = key_value[:, HD:].astype(BF16)
    newk_v[...] = new_key
    newv_v[...] = new_value
    c_newk = copy(newk_v, newk, sem.at[9])
    c_newv = copy(newv_v, newv, sem.at[10])
    pad = jnp.zeros((HD - rows, HD), BF16)

    def attend(query):
        query_rot = jnp.concatenate(
            [head_norm(query[:, g * HD : (g + 1) * HD], qgain_row) for g in range(group)], axis=0
        )
        keys = jnp.concatenate([key_v[...].reshape(cached, HD), new_key, pad], axis=0)
        scores = lax.dot_general(query_rot, keys, last, preferred_element_type=F32) * HD**-0.5
        masked = (scores.reshape(group, rows, spread) + bias).reshape(group * rows, spread)
        top = jnp.max(masked, axis=-1, keepdims=True)
        weight = jnp.exp(masked - top)
        total = jnp.sum(weight, axis=-1, keepdims=True)
        probs = (weight * (1.0 / total)).astype(BF16)
        values = jnp.concatenate([val_v[...].reshape(cached, HD), new_value, pad], axis=0)
        out = dot(probs, values).astype(BF16)
        return jnp.concatenate([out[g * rows : (g + 1) * rows] for g in range(group)], axis=1)

    first = lax.axis_index("tensor") == 0
    out = jnp.where(first, hidden, 0.0)
    c_wq[0].wait()
    start_wo()
    c_key.wait()
    c_val.wait()
    query = dot(normed, wq_v[0])
    attended = []
    for i in range(1, blocks):
        c_wq[i].wait()
        start_wo()
        following = dot(normed, wq_v[i])
        attended.append(attend(query))
        query = following
    for i in range(blocks):
        c_wo[i].wait()
        if i == 0:
            attended.append(attend(query))
        out = out + dot(attended[i], wo_v[i * span : (i + 1) * span])
    part[...] = out.astype(BF16)
    c_newk.wait()
    c_newv.wait()


def section_partial(args):
    state, gain, wq, wk, wv, wo, qgain, kgain, ckey, cval, lens = args
    rows, width = state.shape[1:]
    any_space = pl.BlockSpec(memory_space=pltpu.HBM)
    vmem = pl.BlockSpec(memory_space=pltpu.VMEM)
    slots = ckey.shape[3]
    ckey = ckey.reshape(rows, slots, HD)
    cval = cval.reshape(rows, slots, HD)
    args = (state, gain, wq, wk, wv, wo, qgain, kgain, ckey, cval, lens)
    args = [pltpu.with_memory_space_constraint(a, pltpu.HBM) for a in args]
    return pl.pallas_call(
        kernel,
        out_shape=(
            pltpu.VMEM((rows, width), BF16),
            pltpu.HBM((rows, HD), BF16),
            pltpu.HBM((rows, HD), BF16),
        ),
        in_specs=[any_space] * len(args),
        out_specs=(vmem, any_space, any_space),
        scratch_shapes=[
            pltpu.VMEM(state.shape, BF16),
            pltpu.VMEM(gain.shape, BF16),
            pltpu.VMEM((BLOCKS, width, wq.shape[2] // BLOCKS), BF16),
            pltpu.VMEM((width, 2 * HD), BF16),
            pltpu.VMEM(wo.shape[1:], BF16),
            pltpu.VMEM(qgain.shape, BF16),
            pltpu.VMEM(kgain.shape, BF16),
            pltpu.VMEM(ckey.shape, BF16),
            pltpu.VMEM(cval.shape, BF16),
            pltpu.VMEM(lens.shape, jnp.int32),
            pltpu.VMEM((rows, HD), BF16),
            pltpu.VMEM((rows, HD), BF16),
            pltpu.SemaphoreType.DMA((11,)),
            pltpu.SemaphoreType.DMA((BLOCKS,)),
            pltpu.SemaphoreType.DMA((BLOCKS,)),
        ],
        compiler_params=pltpu.CompilerParams(vmem_limit_bytes=24 * 2**20),
        cost_estimate=pl.CostEstimate(
            flops=2 * rows * (wq.size + wk.size + wv.size + wo.size),
            bytes_accessed=2 * (wq.size + wk.size + wv.size + wo.size + ckey.size + cval.size),
            transcendentals=0,
        ),
    )(*args)


ROUTES = (
    ((0, 2), (1, 1), (0, 0), (1, 3)),
    ((0, 2), (1, 3), (0, 0), (1, 1)),
    ((0, 1), (1, 0), (0, 3), (1, 2)),
    ((0, 1), (1, 2), (0, 3), (1, 0)),
)
SWAP = ((0, 1), (0, 0), (0, 3), (0, 2))


def added(a, b):
    return (a.astype(F32) + b.astype(F32)).astype(BF16)


def body(sections, *args):
    def moved(x, route):
        pairs = [
            (s * len(route) + t, (s + step) % sections * len(route) + to)
            for s in range(sections)
            for t, (step, to) in enumerate(route)
        ]
        return lax.ppermute(x, ("section", "tensor"), pairs)

    part, new_key, new_value = section_partial(args)
    pair = added(part, moved(part, SWAP))
    a, b, c, d = [moved(pair, route) for route in ROUTES]
    odd = lax.axis_index("tensor") % 2 == 1
    handed = jnp.where(odd, added(b, a), added(d, c))
    rows = part.shape[0]
    return handed[None], new_key.reshape(1, rows, 1, HD), new_value.reshape(1, rows, 1, HD)


def solution(mesh):
    placed = (
        P("section", None, None),
        P("section", None),
        P("section", None, "tensor"),
        P("section", None, "tensor"),
        P("section", None, "tensor"),
        P("section", "tensor", None),
        P("section", None),
        P("section", None),
        P("section", None, "tensor", None, None),
        P("section", None, "tensor", None, None),
        P("section", None),
    )
    return jax.shard_map(
        functools.partial(body, mesh.shape["section"]),
        mesh=mesh,
        in_specs=placed,
        out_specs=(
            P("section", None, None),
            P("section", None, "tensor", None),
            P("section", None, "tensor", None),
        ),
        check_vma=False,
    )
```

```python
import functools

import jax
import jax.numpy as jnp
from jax import lax
from jax.experimental import pallas as pl
from jax.experimental.pallas import tpu as pltpu
from jax.sharding import PartitionSpec as P

HD = 128
EPSILON = 1e-06
BLOCKS = 2
LOG_BASE = 13.815510557964274
NEG = -1e30
F32 = jnp.float32
BF16 = jnp.bfloat16


def dot(a, b):
    return jnp.dot(a, b, preferred_element_type=F32)


def kernel(
    state, gain, wq, wk, wv, wo, qgain, kgain, ckey, cval, lens,
    part, newk, newv,
    state_v, gain_v, wq_v, wkv_v, wo_v, qgain_v, kgain_v, key_v, val_v, lens_v, newk_v, newv_v,
    sem, wq_sem, wo_sem,
):
    rows, width = state_v.shape[1:]
    slots = ckey.shape[1]
    cached = rows * slots
    heads = wq.shape[2] // HD
    blocks = BLOCKS
    group = heads // blocks
    span = group * HD
    last = (((1,), (1,)), ((), ()))

    def copy(src, dst, s, priority=0):
        c = pltpu.make_async_copy(src, dst, s)
        c.start(priority=priority)
        return c

    c_state = copy(state, state_v, sem.at[0])
    c_gain = copy(gain, gain_v, sem.at[1])
    c_lens = copy(lens, lens_v, sem.at[2])
    c_qgain = copy(qgain, qgain_v, sem.at[3])
    c_kgain = copy(kgain, kgain_v, sem.at[4])
    c_wk = copy(wk.at[0], wkv_v.at[:, pl.ds(0, HD)], sem.at[5])
    c_wv = copy(wv.at[0], wkv_v.at[:, pl.ds(HD, HD)], sem.at[6])
    c_key = copy(ckey, key_v, sem.at[7])
    c_val = copy(cval, val_v, sem.at[8])
    c_wq = [copy(wq.at[0, :, pl.ds(i * span, span)], wq_v.at[i], wq_sem.at[i]) for i in range(blocks)]

    def fetch_wo(i):
        at = pl.ds(i * span, span)
        return copy(wo.at[0, at], wo_v.at[at], wo_sem.at[i], 1)

    c_wo = [fetch_wo(0)]

    c_lens.wait()
    c_state.wait()
    c_gain.wait()
    c_qgain.wait()
    c_kgain.wait()
    row_i = lax.broadcasted_iota(jnp.int32, (rows, rows), 0)
    row_j = lax.broadcasted_iota(jnp.int32, (rows, rows), 1)
    length = jnp.sum(
        jnp.where(row_i == row_j, lens_v[...].astype(F32), 0.0), axis=1, keepdims=True
    )
    lane = lax.broadcasted_iota(jnp.int32, (rows, HD), 1)
    half = lax.rem(lane, HD // 2).astype(F32)
    angle = length * jnp.exp(half * (-2.0 * LOG_BASE / HD))
    cosine = jnp.cos(angle)
    sine = jnp.sin(angle)
    sine = jnp.where(lane < HD // 2, -sine, sine)
    spread = cached + HD
    at_row = lax.broadcasted_iota(jnp.int32, (rows, spread), 0)
    at_col = lax.broadcasted_iota(jnp.int32, (rows, spread), 1)
    slot = at_col - at_row * slots
    valid = (slot >= 0) & (slot < length.astype(jnp.int32)) & (at_col < cached)
    valid = valid | (at_col == cached + at_row)
    bias = jnp.where(valid, 0.0, NEG)

    hidden = state_v[0].astype(F32)
    mean = jnp.mean(hidden * hidden, axis=-1, keepdims=True)
    normed = (hidden * lax.rsqrt(mean + EPSILON) * gain_v[...].astype(F32)).astype(BF16)
    qgain_row = qgain_v[...].astype(F32)

    def head_norm(x, gain_row):
        mean = jnp.mean(x * x, axis=-1, keepdims=True)
        x = x * lax.rsqrt(mean + EPSILON) * gain_row
        return (x * cosine + pltpu.roll(x, HD // 2, 1) * sine).astype(BF16)

    c_wk.wait()
    c_wv.wait()
    c_wo.extend(fetch_wo(i) for i in range(1, blocks))
    key_value = dot(normed, wkv_v[...])
    new_key = head_norm(key_value[:, :HD], kgain_v[...].astype(F32))
    new_value = key_value[:, HD:].astype(BF16)
    newk_v[...] = new_key
    newv_v[...] = new_value
    c_newk = copy(newk_v, newk, sem.at[9])
    c_newv = copy(newv_v, newv, sem.at[10])
    pad = jnp.zeros((HD - rows, HD), BF16)

    def attend(query):
        query_rot = jnp.concatenate(
            [head_norm(query[:, g * HD : (g + 1) * HD], qgain_row) for g in range(group)], axis=0
        )
        keys = jnp.concatenate([key_v[...].reshape(cached, HD), new_key, pad], axis=0)
        scores = lax.dot_general(query_rot, keys, last, preferred_element_type=F32) * HD**-0.5
        masked = (scores.reshape(group, rows, spread) + bias).reshape(group * rows, spread)
        top = jnp.max(masked, axis=-1, keepdims=True)
        weight = jnp.exp(masked - top)
        total = jnp.sum(weight, axis=-1, keepdims=True)
        probs = (weight * (1.0 / total)).astype(BF16)
        values = jnp.concatenate([val_v[...].reshape(cached, HD), new_value, pad], axis=0)
        out = dot(probs, values).astype(BF16)
        return jnp.concatenate([out[g * rows : (g + 1) * rows] for g in range(group)], axis=1)

    first = lax.axis_index("tensor") == 0
    out = jnp.where(first, hidden, 0.0)
    c_wq[0].wait()
    c_key.wait()
    c_val.wait()
    query = dot(normed, wq_v[0])
    attended = []
    for i in range(1, blocks):
        c_wq[i].wait()
        following = dot(normed, wq_v[i])
        attended.append(attend(query))
        query = following
    attended.append(attend(query))
    for i in range(blocks):
        c_wo[i].wait()
        out = out + dot(attended[i], wo_v[i * span : (i + 1) * span])
    part[...] = out.astype(BF16)
    c_newk.wait()
    c_newv.wait()


def section_partial(args):
    state, gain, wq, wk, wv, wo, qgain, kgain, ckey, cval, lens = args
    rows, width = state.shape[1:]
    any_space = pl.BlockSpec(memory_space=pltpu.HBM)
    vmem = pl.BlockSpec(memory_space=pltpu.VMEM)
    slots = ckey.shape[3]
    ckey = ckey.reshape(rows, slots, HD)
    cval = cval.reshape(rows, slots, HD)
    args = (state, gain, wq, wk, wv, wo, qgain, kgain, ckey, cval, lens)
    args = [pltpu.with_memory_space_constraint(a, pltpu.HBM) for a in args]
    return pl.pallas_call(
        kernel,
        out_shape=(
            pltpu.VMEM((rows, width), BF16),
            pltpu.HBM((rows, HD), BF16),
            pltpu.HBM((rows, HD), BF16),
        ),
        in_specs=[any_space] * len(args),
        out_specs=(vmem, any_space, any_space),
        scratch_shapes=[
            pltpu.VMEM(state.shape, BF16),
            pltpu.VMEM(gain.shape, BF16),
            pltpu.VMEM((BLOCKS, width, wq.shape[2] // BLOCKS), BF16),
            pltpu.VMEM((width, 2 * HD), BF16),
            pltpu.VMEM(wo.shape[1:], BF16),
            pltpu.VMEM(qgain.shape, BF16),
            pltpu.VMEM(kgain.shape, BF16),
            pltpu.VMEM(ckey.shape, BF16),
            pltpu.VMEM(cval.shape, BF16),
            pltpu.VMEM(lens.shape, jnp.int32),
            pltpu.VMEM((rows, HD), BF16),
            pltpu.VMEM((rows, HD), BF16),
            pltpu.SemaphoreType.DMA((11,)),
            pltpu.SemaphoreType.DMA((BLOCKS,)),
            pltpu.SemaphoreType.DMA((BLOCKS,)),
        ],
        compiler_params=pltpu.CompilerParams(vmem_limit_bytes=24 * 2**20),
        cost_estimate=pl.CostEstimate(
            flops=2 * rows * (wq.size + wk.size + wv.size + wo.size),
            bytes_accessed=2 * (wq.size + wk.size + wv.size + wo.size + ckey.size + cval.size),
            transcendentals=0,
        ),
    )(*args)


ROUTES = (
    ((0, 2), (1, 1), (0, 0), (1, 3)),
    ((0, 2), (1, 3), (0, 0), (1, 1)),
    ((0, 1), (1, 0), (0, 3), (1, 2)),
    ((0, 1), (1, 2), (0, 3), (1, 0)),
)
SWAP = ((0, 1), (0, 0), (0, 3), (0, 2))


def added(a, b):
    return (a.astype(F32) + b.astype(F32)).astype(BF16)


def body(sections, *args):
    def moved(x, route):
        pairs = [
            (s * len(route) + t, (s + step) % sections * len(route) + to)
            for s in range(sections)
            for t, (step, to) in enumerate(route)
        ]
        return lax.ppermute(x, ("section", "tensor"), pairs)

    part, new_key, new_value = section_partial(args)
    pair = added(part, moved(part, SWAP))
    a, b, c, d = [moved(pair, route) for route in ROUTES]
    odd = lax.axis_index("tensor") % 2 == 1
    handed = jnp.where(odd, added(b, a), added(d, c))
    rows = part.shape[0]
    return handed[None], new_key.reshape(1, rows, 1, HD), new_value.reshape(1, rows, 1, HD)


def solution(mesh):
    placed = (
        P("section", None, None),
        P("section", None),
        P("section", None, "tensor"),
        P("section", None, "tensor"),
        P("section", None, "tensor"),
        P("section", "tensor", None),
        P("section", None),
        P("section", None),
        P("section", None, "tensor", None, None),
        P("section", None, "tensor", None, None),
        P("section", None),
    )
    return jax.shard_map(
        functools.partial(body, mesh.shape["section"]),
        mesh=mesh,
        in_specs=placed,
        out_specs=(
            P("section", None, None),
            P("section", None, "tensor", None),
            P("section", None, "tensor", None),
        ),
        check_vma=False,
    )
```

```python
import functools

import jax
import jax.numpy as jnp
from jax import lax
from jax.experimental import pallas as pl
from jax.experimental.pallas import tpu as pltpu
from jax.sharding import PartitionSpec as P

HD = 128
EPSILON = 1e-06
BLOCKS = 2
LOG_BASE = 13.815510557964274
NEG = -1e30
F32 = jnp.float32
BF16 = jnp.bfloat16


def dot(a, b):
    return jnp.dot(a, b, preferred_element_type=F32)


def kernel(
    state, gain, wq, wk, wv, wo, qgain, kgain, ckey, cval, lens,
    part, newk, newv,
    state_v, gain_v, wq_v, wkv_v, wo_v, qgain_v, kgain_v, key_v, val_v, lens_v, newk_v, newv_v,
    sem, wq_sem, wo_sem,
):
    rows, width = state_v.shape[1:]
    slots = ckey.shape[1]
    cached = rows * slots
    heads = wq.shape[2] // HD
    blocks = BLOCKS
    group = heads // blocks
    span = group * HD
    last = (((1,), (1,)), ((), ()))

    def copy(src, dst, s, priority=0):
        c = pltpu.make_async_copy(src, dst, s)
        c.start(priority=priority)
        return c

    c_state = copy(state, state_v, sem.at[0])
    c_gain = copy(gain, gain_v, sem.at[1])
    c_lens = copy(lens, lens_v, sem.at[2])
    c_qgain = copy(qgain, qgain_v, sem.at[3])
    c_kgain = copy(kgain, kgain_v, sem.at[4])
    c_wk = copy(wk.at[0], wkv_v.at[:, pl.ds(0, HD)], sem.at[5])
    c_wv = copy(wv.at[0], wkv_v.at[:, pl.ds(HD, HD)], sem.at[6])
    c_key = copy(ckey, key_v, sem.at[7])
    c_val = copy(cval, val_v, sem.at[8])
    c_wq = [copy(wq.at[0, :, pl.ds(i * span, span)], wq_v.at[i], wq_sem.at[i]) for i in range(blocks)]

    def fetch_wo(i):
        at = pl.ds(i * span, span)
        return copy(wo.at[0, at], wo_v.at[at], wo_sem.at[i], 1)

    c_wo = [fetch_wo(0)]

    c_lens.wait()
    c_state.wait()
    c_gain.wait()
    c_qgain.wait()
    c_kgain.wait()
    row_i = lax.broadcasted_iota(jnp.int32, (rows, rows), 0)
    row_j = lax.broadcasted_iota(jnp.int32, (rows, rows), 1)
    length = jnp.sum(
        jnp.where(row_i == row_j, lens_v[...].astype(F32), 0.0), axis=1, keepdims=True
    )
    lane = lax.broadcasted_iota(jnp.int32, (rows, HD), 1)
    half = lax.rem(lane, HD // 2).astype(F32)
    angle = length * jnp.exp(half * (-2.0 * LOG_BASE / HD))
    cosine = jnp.cos(angle)
    sine = jnp.sin(angle)
    sine = jnp.where(lane < HD // 2, -sine, sine)
    spread = cached + HD
    at_row = lax.broadcasted_iota(jnp.int32, (rows, spread), 0)
    at_col = lax.broadcasted_iota(jnp.int32, (rows, spread), 1)
    slot = at_col - at_row * slots
    valid = (slot >= 0) & (slot < length.astype(jnp.int32)) & (at_col < cached)
    valid = valid | (at_col == cached + at_row)
    bias = jnp.where(valid, 0.0, NEG)

    hidden = state_v[0].astype(F32)
    mean = jnp.mean(hidden * hidden, axis=-1, keepdims=True)
    normed = (hidden * lax.rsqrt(mean + EPSILON) * gain_v[...].astype(F32)).astype(BF16)
    qgain_row = qgain_v[...].astype(F32)

    def head_norm(x, gain_row):
        mean = jnp.mean(x * x, axis=-1, keepdims=True)
        x = x * lax.rsqrt(mean + EPSILON) * gain_row
        return (x * cosine + pltpu.roll(x, HD // 2, 1) * sine).astype(BF16)

    c_wk.wait()
    c_wv.wait()
    c_wo.extend(fetch_wo(i) for i in range(1, blocks))
    key_value = dot(normed, wkv_v[...])
    new_key = head_norm(key_value[:, :HD], kgain_v[...].astype(F32))
    new_value = key_value[:, HD:].astype(BF16)
    newk_v[...] = new_key
    newv_v[...] = new_value
    c_newk = copy(newk_v, newk, sem.at[9])
    c_newv = copy(newv_v, newv, sem.at[10])
    pad = jnp.zeros((HD - rows, HD), BF16)

    def attend(query):
        query_rot = jnp.concatenate(
            [head_norm(query[:, g * HD : (g + 1) * HD], qgain_row) for g in range(group)], axis=0
        )
        keys = jnp.concatenate([key_v[...].reshape(cached, HD), new_key, pad], axis=0)
        scores = lax.dot_general(query_rot, keys, last, preferred_element_type=F32) * HD**-0.5
        masked = (scores.reshape(group, rows, spread) + bias).reshape(group * rows, spread)
        top = jnp.max(masked, axis=-1, keepdims=True)
        weight = jnp.exp(masked - top)
        total = jnp.sum(weight, axis=-1, keepdims=True)
        probs = (weight * (1.0 / total)).astype(BF16)
        values = jnp.concatenate([val_v[...].reshape(cached, HD), new_value, pad], axis=0)
        out = dot(probs, values).astype(BF16)
        return jnp.concatenate([out[g * rows : (g + 1) * rows] for g in range(group)], axis=1)

    first = lax.axis_index("tensor") == 0
    out = jnp.where(first, hidden, 0.0)
    c_wq[0].wait()
    c_key.wait()
    c_val.wait()
    query = dot(normed, wq_v[0])
    attended = []
    for i in range(1, blocks):
        c_wq[i].wait()
        following = dot(normed, wq_v[i])
        attended.append(attend(query))
        query = following
    attended.append(attend(query))
    c_wo[0].wait()
    outs = []
    for at in range(0, width, 512):
        outs.append(out[:, at : at + 512] + dot(attended[0], wo_v[:span, at : at + 512]))
    c_wo[1].wait()
    for k, at in enumerate(range(0, width, 512)):
        share = dot(attended[1], wo_v[span:, at : at + 512])
        part[:, at : at + 512] = (outs[k] + share).astype(BF16)
    c_newk.wait()
    c_newv.wait()


def section_partial(args):
    state, gain, wq, wk, wv, wo, qgain, kgain, ckey, cval, lens = args
    rows, width = state.shape[1:]
    any_space = pl.BlockSpec(memory_space=pltpu.HBM)
    vmem = pl.BlockSpec(memory_space=pltpu.VMEM)
    slots = ckey.shape[3]
    ckey = ckey.reshape(rows, slots, HD)
    cval = cval.reshape(rows, slots, HD)
    args = (state, gain, wq, wk, wv, wo, qgain, kgain, ckey, cval, lens)
    args = [pltpu.with_memory_space_constraint(a, pltpu.HBM) for a in args]
    return pl.pallas_call(
        kernel,
        out_shape=(
            pltpu.VMEM((rows, width), BF16),
            pltpu.HBM((rows, HD), BF16),
            pltpu.HBM((rows, HD), BF16),
        ),
        in_specs=[any_space] * len(args),
        out_specs=(vmem, any_space, any_space),
        scratch_shapes=[
            pltpu.VMEM(state.shape, BF16),
            pltpu.VMEM(gain.shape, BF16),
            pltpu.VMEM((BLOCKS, width, wq.shape[2] // BLOCKS), BF16),
            pltpu.VMEM((width, 2 * HD), BF16),
            pltpu.VMEM(wo.shape[1:], BF16),
            pltpu.VMEM(qgain.shape, BF16),
            pltpu.VMEM(kgain.shape, BF16),
            pltpu.VMEM(ckey.shape, BF16),
            pltpu.VMEM(cval.shape, BF16),
            pltpu.VMEM(lens.shape, jnp.int32),
            pltpu.VMEM((rows, HD), BF16),
            pltpu.VMEM((rows, HD), BF16),
            pltpu.SemaphoreType.DMA((11,)),
            pltpu.SemaphoreType.DMA((BLOCKS,)),
            pltpu.SemaphoreType.DMA((BLOCKS,)),
        ],
        compiler_params=pltpu.CompilerParams(vmem_limit_bytes=24 * 2**20),
        cost_estimate=pl.CostEstimate(
            flops=2 * rows * (wq.size + wk.size + wv.size + wo.size),
            bytes_accessed=2 * (wq.size + wk.size + wv.size + wo.size + ckey.size + cval.size),
            transcendentals=0,
        ),
    )(*args)


ROUTES = (
    ((0, 2), (1, 1), (0, 0), (1, 3)),
    ((0, 2), (1, 3), (0, 0), (1, 1)),
    ((0, 1), (1, 0), (0, 3), (1, 2)),
    ((0, 1), (1, 2), (0, 3), (1, 0)),
)
SWAP = ((0, 1), (0, 0), (0, 3), (0, 2))


def added(a, b):
    return (a.astype(F32) + b.astype(F32)).astype(BF16)


def body(sections, *args):
    def moved(x, route):
        pairs = [
            (s * len(route) + t, (s + step) % sections * len(route) + to)
            for s in range(sections)
            for t, (step, to) in enumerate(route)
        ]
        return lax.ppermute(x, ("section", "tensor"), pairs)

    part, new_key, new_value = section_partial(args)
    pair = added(part, moved(part, SWAP))
    a, b, c, d = [moved(pair, route) for route in ROUTES]
    odd = lax.axis_index("tensor") % 2 == 1
    handed = jnp.where(odd, added(b, a), added(d, c))
    rows = part.shape[0]
    return handed[None], new_key.reshape(1, rows, 1, HD), new_value.reshape(1, rows, 1, HD)


def solution(mesh):
    placed = (
        P("section", None, None),
        P("section", None),
        P("section", None, "tensor"),
        P("section", None, "tensor"),
        P("section", None, "tensor"),
        P("section", "tensor", None),
        P("section", None),
        P("section", None),
        P("section", None, "tensor", None, None),
        P("section", None, "tensor", None, None),
        P("section", None),
    )
    return jax.shard_map(
        functools.partial(body, mesh.shape["section"]),
        mesh=mesh,
        in_specs=placed,
        out_specs=(
            P("section", None, None),
            P("section", None, "tensor", None),
            P("section", None, "tensor", None),
        ),
        check_vma=False,
    )
```
